32 devices in a mesh: len: 4 (over y, x), hgt: 4 (over z), wid: 2 (over core).
Axes of the slice: x: 2, y: 2, z: 4, core: 2. Of those that a mesh axis runs over, the one named last changes fastest.
Arguments:
- precursor_velocity: float32 [3, 64, 32, 128], P(None, 'len', 'hgt'), may hold values from -6 to 6
- face_velocity: float32 [3, 64, 32, 256], P(None, 'len', 'hgt', 'wid'), may hold values from -6 to 6
- solid_cells: int32 [64, 32, 256], P('len', 'hgt', 'wid'), may hold values 0 or 1
- inlet_profile: float32 [3, 32], P(None, 'hgt'), may hold values from -6 to 6
- target_spread: float32 [3, 32], P(None, 'hgt'), may hold values from 0.3 to 2
Outputs:
- precursor_next: float32 [3, 64, 32, 128], P(None, 'len', 'hgt')
- face_next: float32 [3, 64, 32, 256], P(None, 'len', 'hgt', 'wid')
The draws below stay inside these ranges and needn't reach their ends.
All inputs are finite; a program needn't handle non-finite values. No bound on the sum of `solid_cells` on one device may be relied on, other than what follows from the above.
Results may differ from the reference program's by a relative error of at most 0.0001.
Values sent between devices are 32-bit elements; how exact they have to be, the bound alone decides.
A program may use at most 64 MiB of HBM per device.

```python
import math
import jax
import jax.numpy as jnp
from jax import lax

PW = 128
STEPS = 3
FLEN = 64
FHT = 32
FWD = 256
PLEN = 64


def place_ends(drawn, rng, smallest, high):
    extent = drawn.shape
    spot = [jax.random.randint(jax.random.fold_in(rng, axis), (), 0, extent[axis]) for axis in range(len(extent))]
    drawn = drawn.at[tuple(spot)].set(smallest)
    longest = extent.index(max(extent))
    spot[longest] = (spot[longest] + 1) % extent[longest]
    return drawn.at[tuple(spot)].set(high)


def block_levels(rng, extent, shards, smallest, high):
    factor_of = 1.0
    for axis_at, parts in shards:
        steps = jax.random.uniform(jax.random.fold_in(jax.random.fold_in(rng, 6), axis_at), (parts,), jnp.float32, smallest / len(shards), high / len(shards))
        factor_of = factor_of * jnp.repeat(jnp.exp(steps), extent[axis_at] // parts).reshape((-1,) + (1,) * (len(extent) - 1 - axis_at))
    return factor_of


def bell_draw(key, shape, spread, bound, shards=(), held_as=jnp.bfloat16):
    drawn = spread * jax.random.normal(key, shape, jnp.float32)
    if shards:
        drawn = drawn * block_levels(key, shape, shards, -0.22, 0.18)
    return jnp.clip(drawn, -bound, bound).astype(held_as)


def setup_inputs(seed: int = 0) -> dict:
    streams_of = jax.random.split(jax.random.key(seed), 6)
    precursor_velocity = bell_draw(streams_of[0], (3, PLEN, FHT, PW), 1.0, 6.0, ((1, 4), (2, 4)), jnp.float32)
    face_velocity = bell_draw(streams_of[1], (3, FLEN, FHT, FWD), 1.0, 6.0, ((1, 4), (2, 4), (3, 2)), jnp.float32)
    solid_cells = place_ends((jax.random.randint(streams_of[2], (FLEN, FHT, FWD), 0, 8) < 1).astype(jnp.int32), jax.random.fold_in(streams_of[2], 1), 0, 1)
    inlet_profile = bell_draw(streams_of[3], (3, FHT), 1.0, 6.0, ((1, 4),), jnp.float32)
    target_spread = jnp.clip(jnp.exp(math.log(2.0) - 1.89712 * jax.random.uniform(streams_of[4], (3, FHT), jnp.float32) ** block_levels(streams_of[4], (3, FHT), ((1, 4),), -0.2, 0.2)), 0.3, 2.0)
    return dict(precursor_velocity=precursor_velocity, face_velocity=face_velocity, solid_cells=solid_cells, inlet_profile=inlet_profile, target_spread=target_spread)


time_step = 0.3
viscosity = 0.04
smag_coef = 0.03
spread_eps = 1e-05

def stencil(velocity, ext_len, ext_hgt, ext_wid):
    extended = (ext_len, ext_hgt, ext_wid)
    gradients = []
    laplacian = jnp.zeros_like(velocity)
    for axis_dim in range(3):
        source = extended[axis_dim]
        total = source.shape[axis_dim + 1]
        upper_side = lax.slice_in_dim(source, 2, total, axis=axis_dim + 1)
        lower_side = lax.slice_in_dim(source, 0, total - 2, axis=axis_dim + 1)
        gradients.append((upper_side - lower_side) * 0.5)
        laplacian = laplacian + upper_side + lower_side - 2.0 * velocity
    strain_sum = jnp.zeros_like(velocity[0])
    for comp in range(3):
        for axis_dim in range(3):
            strain = 0.5 * (gradients[axis_dim][comp] + gradients[comp][axis_dim])
            strain_sum = strain_sum + strain * strain
    strain_norm = jnp.sqrt(2.0 * strain_sum)
    nu_eff = viscosity + smag_coef * strain_norm
    advect = jnp.zeros_like(velocity)
    for axis_dim in range(3):
        advect = advect + velocity[axis_dim][None] * gradients[axis_dim]
    return velocity + time_step * (nu_eff[None] * laplacian - advect)

def rescale_plane(recycled, inlet_profile, target_spread):
    plane_mean = lax.optimization_barrier(jnp.mean(recycled, axis=2, keepdims=True))
    fluctuation = recycled - plane_mean
    plane_spread = jnp.sqrt(lax.optimization_barrier(jnp.mean(fluctuation * fluctuation, axis=2, keepdims=True)) + spread_eps)
    return inlet_profile[:, :, None] + target_spread[:, :, None] / plane_spread * fluctuation

def reference(precursor_velocity, face_velocity, solid_cells, inlet_profile, target_spread):
    precursor = precursor_velocity
    face_zone = face_velocity
    fluid_share = (1 - solid_cells).astype(jnp.float32)
    for step_index in range(STEPS):
        recycled = precursor[:, -1]
        inlet_plane = rescale_plane(recycled, inlet_profile, target_spread)
        inlet_plane = jnp.tile(inlet_plane, (1, 1, FWD // PW))
        pre_len = jnp.concatenate([precursor[:, -1:], precursor, precursor[:, :1]], axis=1)
        pre_hgt = jnp.pad(precursor, ((0, 0), (0, 0), (1, 1), (0, 0)))
        pre_wid = jnp.pad(precursor, ((0, 0), (0, 0), (0, 0), (1, 1)))
        precursor_new = stencil(precursor, pre_len, pre_hgt, pre_wid)
        face_len = jnp.concatenate([inlet_plane[:, None], face_zone, face_zone[:, -1:]], axis=1)
        face_hgt = jnp.pad(face_zone, ((0, 0), (0, 0), (1, 1), (0, 0)))
        face_wid = jnp.pad(face_zone, ((0, 0), (0, 0), (0, 0), (1, 1)))
        face_zone = stencil(face_zone, face_len, face_hgt, face_wid) * fluid_share[None]
        precursor = precursor_new
    return (precursor, face_zone)
```

```python
import functools

import jax
import jax.numpy as jnp
from jax import lax
from jax.experimental import pallas as pl
from jax.experimental.pallas import tpu as pltpu
from jax.sharding import PartitionSpec as P

STEPS = 3
UNROLL = 2

time_step = 0.3
viscosity = 0.04
smag_coef = 0.03
spread_eps = 1e-05


def stencil(u, len_dn, len_up, hgt_dn, hgt_up, wid_dn, wid_up):
    dn, up = (len_dn, hgt_dn, wid_dn), (len_up, hgt_up, wid_up)
    diff = [[up[d][c] - dn[d][c] for d in range(3)] for c in range(3)]
    diag = diff[0][0] * diff[0][0] + diff[1][1] * diff[1][1] + diff[2][2] * diff[2][2]
    s01 = diff[0][1] + diff[1][0]
    s02 = diff[0][2] + diff[2][0]
    s12 = diff[1][2] + diff[2][1]
    total = 2.0 * diag + s01 * s01 + s02 * s02 + s12 * s12
    nu = time_step * viscosity + (0.5 * time_step * smag_coef) * jnp.sqrt(total)
    half = [(0.5 * time_step) * u[d] for d in range(3)]
    out = []
    for c in range(3):
        lap = (up[0][c] + dn[0][c]) + (up[1][c] + dn[1][c]) + (up[2][c] + dn[2][c]) - 6.0 * u[c]
        adv = half[0] * diff[c][0] + half[1] * diff[c][1] + half[2] * diff[c][2]
        out.append(u[c] + nu * lap - adv)
    return out


def kernel(counts, pre_ref, face_ref, solid_ref, prof_ref, spread_ref, pre_out, face_out,
           state, hsend, hrecv, wsend, wrecv, load_sem, send_sem, recv_sem):
    n_len, n_hgt, n_wid = counts
    planes, rows, cols = solid_ref.shape
    me_len, me_hgt, me_wid = lax.axis_index("len"), lax.axis_index("hgt"), lax.axis_index("wid")
    next_len = lax.rem(me_len + 1, n_len)
    prev_len = lax.rem(me_len + n_len - 1, n_len)

    partners = (
        ("len", next_len, None),
        ("len", prev_len, None),
        ("hgt", me_hgt + 1, me_hgt < n_hgt - 1),
        ("hgt", me_hgt - 1, me_hgt > 0),
        ("wid", me_wid + 1, me_wid < n_wid - 1),
        ("wid", me_wid - 1, me_wid > 0),
    )

    def guarded(cond, fn):
        if cond is None:
            fn()
        else:
            pl.when(cond)(fn)

    loads = [
        pltpu.make_async_copy(pre_ref, state.at[0, 0:3, 1:planes + 1], load_sem.at[0]),
        pltpu.make_async_copy(face_ref, state.at[0, 3:6, 1:planes + 1], load_sem.at[1]),
    ]
    for copy in loads:
        copy.start()

    barrier = pltpu.get_barrier_semaphore()
    for axis, target, cond in partners:
        guarded(cond, lambda axis=axis, target=target: pl.semaphore_signal(
            barrier, inc=1, device_id={axis: target}, device_id_type=pl.DeviceIdType.MESH))

    sub = lax.broadcasted_iota(jnp.int32, (rows, cols), 0)
    lane = lax.broadcasted_iota(jnp.int32, (rows, cols), 1)

    zero_rows = jnp.zeros(hrecv.shape[2:], jnp.float32)
    zero_cols = jnp.zeros(wrecv.shape[2:], jnp.float32)

    def zero(ref, side, value):
        def go():
            for s in range(STEPS):
                ref[s, side] = value
        return go

    pl.when(me_hgt == 0)(zero(hrecv, 0, zero_rows))
    pl.when(me_hgt == n_hgt - 1)(zero(hrecv, 1, zero_rows))
    pl.when(me_wid == 0)(zero(wrecv, 0, zero_cols))
    pl.when(me_wid == n_wid - 1)(zero(wrecv, 1, zero_cols))

    pick = lax.broadcasted_iota(jnp.int32, (rows, rows), 0) == lax.broadcasted_iota(jnp.int32, (rows, rows), 1)

    def column(ref, c):
        return jnp.sum(jnp.where(pick, jnp.broadcast_to(ref[c:c + 1, :], (rows, rows)), 0.0), axis=1, keepdims=True)

    profile = [column(prof_ref, c) for c in range(3)]
    target_spread = [column(spread_ref, c) for c in range(3)]

    def copies(s):
        srcs = [state.at[s, :, planes], state.at[s, :, 1], hsend.at[s, 1], hsend.at[s, 0], wsend.at[s], wsend.at[s]]
        dsts = [state.at[s, :, 0], state.at[s, :, planes + 1], hrecv.at[s, 0], hrecv.at[s, 1], wrecv.at[s, 0], wrecv.at[s, 1]]
        return [
            pltpu.make_async_remote_copy(
                src_ref=srcs[k], dst_ref=dsts[k], send_sem=send_sem.at[s, k], recv_sem=recv_sem.at[s, k],
                device_id={partners[k][0]: partners[k][1]}, device_id_type=pl.DeviceIdType.MESH)
            for k in range(6)
        ]

    def pack(s, l, pre, face, acc):
        for c, x in enumerate(list(pre) + list(face)):
            hsend[s, 0, c, pl.ds(l, 1), :] = x[0:1]
            hsend[s, 1, c, pl.ds(l, 1), :] = x[rows - 1:rows]
        mine = (lane >> 1) == l
        return [jnp.where(mine, pltpu.roll(face[c], 2 * l + 1, 1), acc[c]) for c in range(3)]

    for copy in loads:
        copy.wait()
    no_acc = [jnp.zeros((rows, cols), jnp.float32)] * 3

    def first(l, acc):
        x = [state[0, c, l + 1] for c in range(6)]
        return pack(0, l, x[:3], x[3:], acc)

    acc = lax.fori_loop(0, planes, first, no_acc, unroll=UNROLL)
    for c in range(3):
        wsend[0, c] = acc[c]

    expected = sum([jnp.int32(1) if cond is None else cond.astype(jnp.int32) for _, _, cond in partners])
    pl.semaphore_wait(barrier, expected)

    arrives = (None, None, me_hgt > 0, me_hgt < n_hgt - 1, me_wid > 0, me_wid < n_wid - 1)
    even = (lane & 1) == 0
    for s in range(STEPS):
        sends = copies(s)
        for k in range(6):
            guarded(partners[k][2], sends[k].start)
        for k in range(6):
            guarded(arrives[k], sends[k].wait_recv)
        for c in range(3):
            recycled = state[s, c, 0]
            mean = jnp.sum(recycled, axis=1, keepdims=True) * (1.0 / cols)
            fluct = recycled - mean
            var = jnp.sum(fluct * fluct, axis=1, keepdims=True) * (1.0 / cols)
            inlet = profile[c] + target_spread[c] / jnp.sqrt(var + spread_eps) * fluct
            state[s, 3 + c, 0] = jnp.where(me_len == 0, inlet, state[s, 3 + c, 0])
            state[s, 3 + c, planes + 1] = jnp.where(
                me_len == n_len - 1, state[s, 3 + c, planes], state[s, 3 + c, planes + 1])
        ghosts = [
            jnp.where(even, pltpu.roll(wrecv[s, 1, c], cols - 1, 1), pltpu.roll(wrecv[s, 0, c], 1, 1))
            for c in range(3)
        ]

        def plane(l, acc, s=s, ghosts=ghosts):
            def zone(z):
                u = [state[s, 3 * z + c, l + 1] for c in range(3)]
                len_dn = [state[s, 3 * z + c, l] for c in range(3)]
                len_up = [state[s, 3 * z + c, l + 2] for c in range(3)]
                hgt_dn = [jnp.where(sub == 0, hrecv[s, 0, 3 * z + c, pl.ds(l, 1), :], pltpu.roll(u[c], 1, 0)) for c in range(3)]
                hgt_up = [jnp.where(sub == rows - 1, hrecv[s, 1, 3 * z + c, pl.ds(l, 1), :], pltpu.roll(u[c], rows - 1, 0)) for c in range(3)]
                if z == 0:
                    edge = [0.0] * 3
                else:
                    edge = [pltpu.roll(ghosts[c], cols - (2 * l + 1), 1) for c in range(3)]
                wid_dn = [jnp.where(lane == 0, edge[c], pltpu.roll(u[c], 1, 1)) for c in range(3)]
                wid_up = [jnp.where(lane == cols - 1, edge[c], pltpu.roll(u[c], cols - 1, 1)) for c in range(3)]
                return stencil(u, len_dn, len_up, hgt_dn, hgt_up, wid_dn, wid_up)

            pre = zone(0)
            share = (1 - solid_ref[l]).astype(jnp.float32)
            face = [x * share for x in zone(1)]
            if s == STEPS - 1:
                for c in range(3):
                    pre_out[c, l] = pre[c]
                    face_out[c, l] = face[c]
                return acc
            for c in range(3):
                state[s + 1, c, l + 1] = pre[c]
                state[s + 1, 3 + c, l + 1] = face[c]
            return pack(s + 1, l, pre, face, acc)

        acc = lax.fori_loop(0, planes, plane, no_acc, unroll=UNROLL)
        if s < STEPS - 1:
            for c in range(3):
                wsend[s + 1, c] = acc[c]

    for s in range(STEPS):
        sends = copies(s)
        for k in range(6):
            guarded(partners[k][2], sends[k].wait_send)


def on_device(counts, precursor, face, solid, inlet_profile, target_spread):
    planes, rows, cols = solid.shape
    vmem = pl.BlockSpec(memory_space=pltpu.VMEM)
    hbm = pl.BlockSpec(memory_space=pl.ANY)
    f32 = jnp.float32
    return pl.pallas_call(
        functools.partial(kernel, counts),
        out_shape=(jax.ShapeDtypeStruct(precursor.shape, f32), jax.ShapeDtypeStruct(face.shape, f32)),
        in_specs=[hbm, hbm, vmem, vmem, vmem],
        out_specs=(vmem, vmem),
        scratch_shapes=[
            pltpu.VMEM((STEPS, 6, planes + 2, rows, cols), f32),
            pltpu.VMEM((STEPS, 2, 6, planes, cols), f32),
            pltpu.VMEM((STEPS, 2, 6, planes, cols), f32),
            pltpu.VMEM((STEPS, 3, rows, cols), f32),
            pltpu.VMEM((STEPS, 2, 3, rows, cols), f32),
            pltpu.SemaphoreType.DMA((2,)),
            pltpu.SemaphoreType.DMA((STEPS, 6)),
            pltpu.SemaphoreType.DMA((STEPS, 6)),
        ],
        compiler_params=pltpu.CompilerParams(
            collective_id=0, has_side_effects=True, vmem_limit_bytes=16 * 1024 * 1024),
    )(precursor, face, solid, inlet_profile, target_spread)


def solution(mesh):
    counts = (mesh.shape["len"], mesh.shape["hgt"], mesh.shape["wid"])
    return jax.shard_map(
        functools.partial(on_device, counts),
        mesh=mesh,
        in_specs=(
            P(None, "len", "hgt", None),
            P(None, "len", "hgt", "wid"),
            P("len", "hgt", "wid"),
            P(None, "hgt"),
            P(None, "hgt"),
        ),
        out_specs=(P(None, "len", "hgt", None), P(None, "len", "hgt", "wid")),
        check_vma=False,
    )
```

```python
import functools

import jax
import jax.numpy as jnp
from jax import lax
from jax.experimental import pallas as pl
from jax.experimental.pallas import tpu as pltpu
from jax.sharding import PartitionSpec as P

STEPS = 3
UNROLL = 16
REMOTE = True

time_step = 0.3
viscosity = 0.04
smag_coef = 0.03
spread_eps = 1e-05


def stencil(u, len_dn, len_up, hgt_dn, hgt_up, wid_dn, wid_up):
    dn, up = (len_dn, hgt_dn, wid_dn), (len_up, hgt_up, wid_up)
    diff = [[up[d][c] - dn[d][c] for d in range(3)] for c in range(3)]
    diag = diff[0][0] * diff[0][0] + diff[1][1] * diff[1][1] + diff[2][2] * diff[2][2]
    s01 = diff[0][1] + diff[1][0]
    s02 = diff[0][2] + diff[2][0]
    s12 = diff[1][2] + diff[2][1]
    total = 2.0 * diag + s01 * s01 + s02 * s02 + s12 * s12
    nu = time_step * viscosity + (0.5 * time_step * smag_coef) * jnp.sqrt(total)
    half = [(0.5 * time_step) * u[d] for d in range(3)]
    out = []
    for c in range(3):
        lap = (up[0][c] + dn[0][c]) + (up[1][c] + dn[1][c]) + (up[2][c] + dn[2][c]) - 6.0 * u[c]
        adv = half[0] * diff[c][0] + half[1] * diff[c][1] + half[2] * diff[c][2]
        out.append(u[c] + nu * lap - adv)
    return out


def kernel(counts, pre_hbm, face_hbm, solid_hbm, prof_hbm, spread_hbm, pre_out, face_out,
           state, solid_ref, prof_ref, spread_ref, hsend, hrecv, wsend, wrecv, load_sem, send_sem, recv_sem):
    n_len, n_hgt, n_wid = counts
    planes, rows, cols = solid_ref.shape
    me_len, me_hgt, me_wid = lax.axis_index("len"), lax.axis_index("hgt"), lax.axis_index("wid")
    next_len = lax.rem(me_len + 1, n_len)
    prev_len = lax.rem(me_len + n_len - 1, n_len)

    partners = (
        ("len", next_len, None),
        ("len", prev_len, None),
        ("hgt", me_hgt + 1, me_hgt < n_hgt - 1),
        ("hgt", me_hgt - 1, me_hgt > 0),
        ("wid", me_wid + 1, me_wid < n_wid - 1),
        ("wid", me_wid - 1, me_wid > 0),
    )
    arrives = (None, None, me_hgt > 0, me_hgt < n_hgt - 1, me_wid > 0, me_wid < n_wid - 1)

    def guarded(cond, fn):
        if cond is None:
            fn()
        else:
            pl.when(cond)(fn)

    if REMOTE:
        barrier = pltpu.get_barrier_semaphore()
        for axis, target, cond in partners:
            guarded(cond, lambda axis=axis, target=target: pl.semaphore_signal(
                barrier, inc=1, device_id={axis: target}, device_id_type=pl.DeviceIdType.MESH))

    loads = [
        pltpu.make_async_copy(src, dst, load_sem.at[k])
        for k, (src, dst) in enumerate((
            (pre_hbm, state.at[0, 0, :, 1:planes + 1]),
            (face_hbm, state.at[0, 1, :, 1:planes + 1]),
            (prof_hbm, prof_ref),
            (spread_hbm, spread_ref),
            (solid_hbm, solid_ref),
        ))
    ]
    for copy in loads:
        copy.start()

    sub = lax.broadcasted_iota(jnp.int32, (rows, cols), 0)
    lane = lax.broadcasted_iota(jnp.int32, (rows, cols), 1)

    zero_rows = jnp.zeros(hrecv.shape[3:], jnp.float32)
    zero_cols = jnp.zeros(wrecv.shape[2:], jnp.float32)

    def no_rows(side):
        def go():
            for s in range(STEPS):
                for z in range(2):
                    hrecv[s, z, side] = zero_rows
        return go

    def no_cols(side):
        def go():
            for s in range(STEPS):
                wrecv[s, side] = zero_cols
        return go

    pl.when(me_hgt == 0)(no_rows(0))
    pl.when(me_hgt == n_hgt - 1)(no_rows(1))
    pl.when(me_wid == 0)(no_cols(0))
    pl.when(me_wid == n_wid - 1)(no_cols(1))

    def copies(s, z):
        pairs = [
            (state.at[s, z, :, planes], state.at[s, z, :, 0]),
            (state.at[s, z, :, 1], state.at[s, z, :, planes + 1]),
            (hsend.at[s, z, 1], hrecv.at[s, z, 0]),
            (hsend.at[s, z, 0], hrecv.at[s, z, 1]),
        ]
        if z == 1:
            pairs += [(wsend.at[s], wrecv.at[s, 0]), (wsend.at[s], wrecv.at[s, 1])]
        return [
            pltpu.make_async_remote_copy(
                src_ref=src, dst_ref=dst, send_sem=send_sem.at[s, z, k], recv_sem=recv_sem.at[s, z, k],
                device_id={partners[k][0]: partners[k][1]}, device_id_type=pl.DeviceIdType.MESH)
            for k, (src, dst) in enumerate(pairs)
        ]

    def start(s, z):
        if REMOTE:
            sends = copies(s, z)
            for k in reversed(range(len(sends))):
                guarded(partners[k][2], sends[k].start)

    def wait_recv(s, z):
        if REMOTE:
            for k, copy in enumerate(copies(s, z)):
                guarded(arrives[k], copy.wait_recv)

    def pack(s, z, l, x, acc):
        for c in range(3):
            hsend[s, z, 0, c, pl.ds(l, 1), :] = x[c][0:1]
            hsend[s, z, 1, c, pl.ds(l, 1), :] = x[c][rows - 1:rows]
        if z == 0:
            return acc
        mine = (lane >> 1) == l
        return [jnp.where(mine, pltpu.roll(x[c], 2 * l + 1, 1), acc[c]) for c in range(3)]

    def empty(z):
        return [jnp.zeros((rows, cols), jnp.float32)] * 3 if z == 1 else []

    def send(s, z, acc):
        for c, x in enumerate(acc):
            wsend[s, c] = x
        start(s, z)

    for z in range(2):
        loads[z].wait()

        def first(l, acc, z=z):
            return pack(0, z, l, [state[0, z, c, l + 1] for c in range(3)], acc)

        acc = lax.fori_loop(0, planes, first, empty(z), unroll=UNROLL)
        if z == 0 and REMOTE:
            expected = sum([jnp.int32(1) if cond is None else cond.astype(jnp.int32) for _, _, cond in partners])
            pl.semaphore_wait(barrier, expected)
        send(0, z, acc)

    for copy in loads[2:]:
        copy.wait()

    pick = lax.broadcasted_iota(jnp.int32, (rows, rows), 0) == lax.broadcasted_iota(jnp.int32, (rows, rows), 1)

    def column(ref, c):
        return jnp.sum(jnp.where(pick, jnp.broadcast_to(ref[c:c + 1, :], (rows, rows)), 0.0), axis=1, keepdims=True)

    profile = [column(prof_ref, c) for c in range(3)]
    target_spread = [column(spread_ref, c) for c in range(3)]

    even = (lane & 1) == 0
    for s in range(STEPS):
        for z in range(2):
            if z == 1:
                inlet = []
                for c in range(3):
                    recycled = state[s, 0, c, 0]
                    mean = jnp.sum(recycled, axis=1, keepdims=True) * (1.0 / cols)
                    fluct = recycled - mean
                    var = jnp.sum(fluct * fluct, axis=1, keepdims=True) * (1.0 / cols)
                    inlet.append(profile[c] + target_spread[c] / jnp.sqrt(var + spread_eps) * fluct)
            wait_recv(s, z)
            ghosts = []
            if z == 1:
                for c in range(3):
                    state[s, 1, c, 0] = jnp.where(me_len == 0, inlet[c], state[s, 1, c, 0])
                    state[s, 1, c, planes + 1] = jnp.where(
                        me_len == n_len - 1, state[s, 1, c, planes], state[s, 1, c, planes + 1])
                    ghosts.append(jnp.where(
                        even, pltpu.roll(wrecv[s, 1, c], cols - 1, 1), pltpu.roll(wrecv[s, 0, c], 1, 1)))

            def plane(l, acc, s=s, z=z, ghosts=ghosts):
                u = [state[s, z, c, l + 1] for c in range(3)]
                len_dn = [state[s, z, c, l] for c in range(3)]
                len_up = [state[s, z, c, l + 2] for c in range(3)]
                hgt_dn = [jnp.where(sub == 0, hrecv[s, z, 0, c, pl.ds(l, 1), :], pltpu.roll(u[c], 1, 0)) for c in range(3)]
                hgt_up = [jnp.where(sub == rows - 1, hrecv[s, z, 1, c, pl.ds(l, 1), :], pltpu.roll(u[c], rows - 1, 0)) for c in range(3)]
                edge = [pltpu.roll(ghosts[c], cols - (2 * l + 1), 1) if z == 1 else 0.0 for c in range(3)]
                wid_dn = [jnp.where(lane == 0, edge[c], pltpu.roll(u[c], 1, 1)) for c in range(3)]
                wid_up = [jnp.where(lane == cols - 1, edge[c], pltpu.roll(u[c], cols - 1, 1)) for c in range(3)]
                x = stencil(u, len_dn, len_up, hgt_dn, hgt_up, wid_dn, wid_up)
                if z == 1:
                    share = (1 - solid_ref[l]).astype(jnp.float32)
                    x = [v * share for v in x]
                for c in range(3):
                    if s == STEPS - 1:
                        (pre_out, face_out)[z][c, l] = x[c]
                    else:
                        state[s + 1, z, c, l + 1] = x[c]
                return acc if s == STEPS - 1 else pack(s + 1, z, l, x, acc)

            acc = lax.fori_loop(0, planes, plane, empty(z), unroll=UNROLL)
            if s < STEPS - 1:
                send(s + 1, z, acc)

    if REMOTE:
        for s in range(STEPS):
            for z in range(2):
                for k, copy in enumerate(copies(s, z)):
                    guarded(partners[k][2], copy.wait_send)


def on_device(counts, precursor, face, solid, inlet_profile, target_spread):
    planes, rows, cols = solid.shape
    vmem = pl.BlockSpec(memory_space=pltpu.VMEM)
    hbm = pl.BlockSpec(memory_space=pltpu.HBM)
    f32 = jnp.float32
    return pl.pallas_call(
        functools.partial(kernel, counts),
        out_shape=(jax.ShapeDtypeStruct(precursor.shape, f32), jax.ShapeDtypeStruct(face.shape, f32)),
        in_specs=[hbm] * 5,
        out_specs=(vmem, vmem),
        scratch_shapes=[
            pltpu.VMEM((STEPS, 2, 3, planes + 2, rows, cols), f32),
            pltpu.VMEM(solid.shape, solid.dtype),
            pltpu.VMEM(inlet_profile.shape, f32),
            pltpu.VMEM(target_spread.shape, f32),
            pltpu.VMEM((STEPS, 2, 2, 3, planes, cols), f32),
            pltpu.VMEM((STEPS, 2, 2, 3, planes, cols), f32),
            pltpu.VMEM((STEPS, 3, rows, cols), f32),
            pltpu.VMEM((STEPS, 2, 3, rows, cols), f32),
            pltpu.SemaphoreType.DMA((5,)),
            pltpu.SemaphoreType.DMA((STEPS, 2, 6)),
            pltpu.SemaphoreType.DMA((STEPS, 2, 6)),
        ],
        compiler_params=pltpu.CompilerParams(
            collective_id=0 if REMOTE else None, has_side_effects=True, vmem_limit_bytes=56 * 1024 * 1024),
    )(precursor, face, solid, inlet_profile, target_spread)


def solution(mesh):
    counts = (mesh.shape["len"], mesh.shape["hgt"], mesh.shape["wid"])
    return jax.shard_map(
        functools.partial(on_device, counts),
        mesh=mesh,
        in_specs=(
            P(None, "len", "hgt", None),
            P(None, "len", "hgt", "wid"),
            P("len", "hgt", "wid"),
            P(None, "hgt"),
            P(None, "hgt"),
        ),
        out_specs=(P(None, "len", "hgt", None), P(None, "len", "hgt", "wid")),
        check_vma=False,
    )
```

```python
import functools

import jax
import jax.numpy as jnp
from jax import lax
from jax.experimental import pallas as pl
from jax.experimental.pallas import tpu as pltpu
from jax.sharding import PartitionSpec as P

STEPS = 3
PARTS = (1, 2)
REMOTE = True

time_step = 0.3
viscosity = 0.04
smag_coef = 0.03
spread_eps = 1e-05


def stencil(u, len_dn, len_up, hgt_dn, hgt_up, wid_dn, wid_up):
    dn, up = (len_dn, hgt_dn, wid_dn), (len_up, hgt_up, wid_up)
    diff = [[up[d][c] - dn[d][c] for d in range(3)] for c in range(3)]
    diag = diff[0][0] * diff[0][0] + diff[1][1] * diff[1][1] + diff[2][2] * diff[2][2]
    s01 = diff[0][1] + diff[1][0]
    s02 = diff[0][2] + diff[2][0]
    s12 = diff[1][2] + diff[2][1]
    total = 2.0 * diag + s01 * s01 + s02 * s02 + s12 * s12
    nu = time_step * viscosity + (0.5 * time_step * smag_coef) * jnp.sqrt(total)
    half = [(0.5 * time_step) * u[d] for d in range(3)]
    out = []
    for c in range(3):
        lap = (up[0][c] + dn[0][c]) + (up[1][c] + dn[1][c]) + (up[2][c] + dn[2][c]) - 6.0 * u[c]
        adv = half[0] * diff[c][0] + half[1] * diff[c][1] + half[2] * diff[c][2]
        out.append(u[c] + nu * lap - adv)
    return out


def kernel(counts, pre_hbm, face_hbm, solid_hbm, prof_hbm, spread_hbm, pre_out, face_out,
           state, solid_ref, prof_ref, spread_ref, hsend, hrecv, wsend, wrecv, load_sem, out_sem, send_sem, recv_sem):
    n_len, n_hgt, n_wid = counts
    planes, rows, cols = solid_ref.shape
    me_len, me_hgt, me_wid = lax.axis_index("len"), lax.axis_index("hgt"), lax.axis_index("wid")
    next_len = lax.rem(me_len + 1, n_len)
    prev_len = lax.rem(me_len + n_len - 1, n_len)

    partners = (
        ("len", next_len, None),
        ("len", prev_len, None),
        ("hgt", me_hgt + 1, me_hgt < n_hgt - 1),
        ("hgt", me_hgt - 1, me_hgt > 0),
        ("wid", me_wid + 1, me_wid < n_wid - 1),
        ("wid", me_wid - 1, me_wid > 0),
    )
    arrives = (None, None, me_hgt > 0, me_hgt < n_hgt - 1, me_wid > 0, me_wid < n_wid - 1)

    def guarded(cond, fn):
        if cond is None:
            fn()
        else:
            pl.when(cond)(fn)

    if REMOTE:
        barrier = pltpu.get_barrier_semaphore()
        for axis, target, cond in partners:
            guarded(cond, lambda axis=axis, target=target: pl.semaphore_signal(
                barrier, inc=1, device_id={axis: target}, device_id_type=pl.DeviceIdType.MESH))

    loads = [
        pltpu.make_async_copy(src, dst, load_sem.at[k])
        for k, (src, dst) in enumerate((
            (pre_hbm, state.at[0, 0, :, 1:planes + 1]),
            (face_hbm, state.at[0, 1, :, 1:planes + 1]),
            (prof_hbm, prof_ref),
            (spread_hbm, spread_ref),
            (solid_hbm, solid_ref),
        ))
    ]
    for copy in loads:
        copy.start()

    sub = lax.broadcasted_iota(jnp.int32, (rows, cols), 0)
    lane = lax.broadcasted_iota(jnp.int32, (rows, cols), 1)

    zero_rows = jnp.zeros(hrecv.shape[3:], jnp.float32)
    zero_cols = jnp.zeros(wrecv.shape[2:], jnp.float32)

    def no_rows(side):
        def go():
            for s in range(STEPS):
                for z in range(2):
                    hrecv[s, z, side] = zero_rows
        return go

    def no_cols(side):
        def go():
            for s in range(STEPS):
                wrecv[s, side] = zero_cols
        return go

    pl.when(me_hgt == 0)(no_rows(0))
    pl.when(me_hgt == n_hgt - 1)(no_rows(1))
    pl.when(me_wid == 0)(no_cols(0))
    pl.when(me_wid == n_wid - 1)(no_cols(1))

    def copies(s, z):
        pairs = [
            (state.at[s, z, :, planes], state.at[s, z, :, 0]),
            (state.at[s, z, :, 1], state.at[s, z, :, planes + 1]),
            (hsend.at[s, z, 1], hrecv.at[s, z, 0]),
            (hsend.at[s, z, 0], hrecv.at[s, z, 1]),
        ]
        if z == 1:
            pairs += [(wsend.at[s], wrecv.at[s, 0]), (wsend.at[s], wrecv.at[s, 1])]
        return [
            pltpu.make_async_remote_copy(
                src_ref=src, dst_ref=dst, send_sem=send_sem.at[s, z, k], recv_sem=recv_sem.at[s, z, k],
                device_id={partners[k][0]: partners[k][1]}, device_id_type=pl.DeviceIdType.MESH)
            for k, (src, dst) in enumerate(pairs)
        ]

    def start(s, z, first, last):
        if REMOTE:
            for k, copy in enumerate(copies(s, z)):
                if first <= k < last:
                    guarded(partners[k][2], copy.start)

    def wait_recv(s, z):
        if REMOTE:
            for k, copy in enumerate(copies(s, z)):
                guarded(arrives[k], copy.wait_recv)

    def pack(s, z, l, x, acc):
        for c in range(3):
            hsend[s, z, 0, c, pl.ds(l, 1), :] = x[c][0:1]
            hsend[s, z, 1, c, pl.ds(l, 1), :] = x[c][rows - 1:rows]
        if z == 0:
            return acc
        mine = (lane >> 1) == l
        return [jnp.where(mine, pltpu.roll(x[c], 2 * l + 1, 1), acc[c]) for c in range(3)]

    def empty(z):
        return [jnp.zeros((rows, cols), jnp.float32)] * 3 if z == 1 else []

    def send(s, z, acc):
        for c, x in enumerate(acc):
            wsend[s, c] = x
        start(s, z, 2, 6)

    for z in range(2):
        loads[z].wait()

        def first(l, acc, z=z):
            return pack(0, z, l, [state[0, z, c, l + 1] for c in range(3)], acc)

        acc = lax.fori_loop(0, planes, first, empty(z), unroll=True)
        for c, x in enumerate(acc):
            wsend[0, c] = x

    if REMOTE:
        expected = sum([jnp.int32(1) if cond is None else cond.astype(jnp.int32) for _, _, cond in partners])
        pl.semaphore_wait(barrier, expected)
    for z in range(2):
        start(0, z, 0, 6)

    for copy in loads[2:]:
        copy.wait()

    pick = lax.broadcasted_iota(jnp.int32, (rows, rows), 0) == lax.broadcasted_iota(jnp.int32, (rows, rows), 1)

    def column(ref, c):
        return jnp.sum(jnp.where(pick, jnp.broadcast_to(ref[c:c + 1, :], (rows, rows)), 0.0), axis=1, keepdims=True)

    profile = [column(prof_ref, c) for c in range(3)]
    target_spread = [column(spread_ref, c) for c in range(3)]

    def result(z, p):
        part = planes // PARTS[z]
        return pltpu.make_async_copy(
            state.at[STEPS, z, :, p * part + 1:(p + 1) * part + 1],
            (pre_out, face_out)[z].at[:, p * part:(p + 1) * part], out_sem.at[z, p])

    even = (lane & 1) == 0
    for s in range(STEPS):
        for z in range(2):
            if z == 1:
                inlet = []
                for c in range(3):
                    recycled = state[s, 0, c, 0]
                    mean = jnp.sum(recycled, axis=1, keepdims=True) * (1.0 / cols)
                    fluct = recycled - mean
                    var = jnp.sum(fluct * fluct, axis=1, keepdims=True) * (1.0 / cols)
                    inlet.append(profile[c] + target_spread[c] / jnp.sqrt(var + spread_eps) * fluct)
            wait_recv(s, z)
            ghosts = []
            if z == 1:
                for c in range(3):
                    state[s, 1, c, 0] = jnp.where(me_len == 0, inlet[c], state[s, 1, c, 0])
                    state[s, 1, c, planes + 1] = jnp.where(
                        me_len == n_len - 1, state[s, 1, c, planes], state[s, 1, c, planes + 1])
                    ghosts.append(jnp.where(
                        even, pltpu.roll(wrecv[s, 1, c], cols - 1, 1), pltpu.roll(wrecv[s, 0, c], 1, 1)))

            def plane(l, acc, s=s, z=z, ghosts=ghosts):
                u = [state[s, z, c, l + 1] for c in range(3)]
                len_dn = [state[s, z, c, l] for c in range(3)]
                len_up = [state[s, z, c, l + 2] for c in range(3)]
                hgt_dn = [jnp.where(sub == 0, hrecv[s, z, 0, c, pl.ds(l, 1), :], pltpu.roll(u[c], 1, 0)) for c in range(3)]
                hgt_up = [jnp.where(sub == rows - 1, hrecv[s, z, 1, c, pl.ds(l, 1), :], pltpu.roll(u[c], rows - 1, 0)) for c in range(3)]
                edge = [pltpu.roll(ghosts[c], cols - (2 * l + 1), 1) if z == 1 else 0.0 for c in range(3)]
                wid_dn = [jnp.where(lane == 0, edge[c], pltpu.roll(u[c], 1, 1)) for c in range(3)]
                wid_up = [jnp.where(lane == cols - 1, edge[c], pltpu.roll(u[c], cols - 1, 1)) for c in range(3)]
                x = stencil(u, len_dn, len_up, hgt_dn, hgt_up, wid_dn, wid_up)
                if z == 1:
                    share = (1 - solid_ref[l]).astype(jnp.float32)
                    x = [v * share for v in x]
                for c in range(3):
                    state[s + 1, z, c, l + 1] = x[c]
                return acc if s == STEPS - 1 else pack(s + 1, z, l, x, acc)

            if s < STEPS - 1:
                acc = plane(planes - 1, plane(0, empty(z)))
                start(s + 1, z, 0, 2)
                acc = lax.fori_loop(1, planes - 1, plane, acc, unroll=True)
                send(s + 1, z, acc)
            else:
                part = planes // PARTS[z]
                for p in range(PARTS[z]):
                    lax.fori_loop(p * part, (p + 1) * part, plane, empty(z), unroll=True)
                    result(z, p).start()

    for z in range(2):
        for p in range(PARTS[z]):
            result(z, p).wait()
    if REMOTE:
        for s in range(STEPS):
            for z in range(2):
                for k, copy in enumerate(copies(s, z)):
                    guarded(partners[k][2], copy.wait_send)


def copy_kernel(pre_in, face_in, pre_out, face_out, held, in_sem, out_sem):
    pairs = ((pre_in, pre_out), (face_in, face_out))
    loads = [pltpu.make_async_copy(src.at[c], held.at[z, c], in_sem.at[z, c])
             for z, (src, _) in enumerate(pairs) for c in range(3)]
    stores = [pltpu.make_async_copy(held.at[z, c], dst.at[c], out_sem.at[z, c])
              for z, (_, dst) in enumerate(pairs) for c in range(3)]
    for load in loads:
        load.start()
    for load, store in zip(loads, stores):
        load.wait()
        store.start()
    for store in stores:
        store.wait()


def on_device(counts, precursor, face, solid, inlet_profile, target_spread):
    planes, rows, cols = solid.shape
    hbm = pl.BlockSpec(memory_space=pltpu.HBM)
    f32 = jnp.float32
    results = pl.pallas_call(
        functools.partial(kernel, counts),
        out_shape=(jax.ShapeDtypeStruct(precursor.shape, f32), jax.ShapeDtypeStruct(face.shape, f32)),
        in_specs=[hbm] * 5,
        out_specs=(hbm, hbm),
        scratch_shapes=[
            pltpu.VMEM((STEPS + 1, 2, 3, planes + 2, rows, cols), f32),
            pltpu.VMEM(solid.shape, solid.dtype),
            pltpu.VMEM(inlet_profile.shape, f32),
            pltpu.VMEM(target_spread.shape, f32),
            pltpu.VMEM((STEPS, 2, 2, 3, planes, cols), f32),
            pltpu.VMEM((STEPS, 2, 2, 3, planes, cols), f32),
            pltpu.VMEM((STEPS, 3, rows, cols), f32),
            pltpu.VMEM((STEPS, 2, 3, rows, cols), f32),
            pltpu.SemaphoreType.DMA((5,)),
            pltpu.SemaphoreType.DMA((2, 4)),
            pltpu.SemaphoreType.DMA((STEPS, 2, 6)),
            pltpu.SemaphoreType.DMA((STEPS, 2, 6)),
        ],
        compiler_params=pltpu.CompilerParams(
            collective_id=0 if REMOTE else None, has_side_effects=True, vmem_limit_bytes=56 * 1024 * 1024),
    )(precursor, face, solid, inlet_profile, target_spread)
    return pl.pallas_call(
        copy_kernel,
        out_shape=(jax.ShapeDtypeStruct(precursor.shape, f32), jax.ShapeDtypeStruct(face.shape, f32)),
        in_specs=[hbm] * 2,
        out_specs=(hbm, hbm),
        scratch_shapes=[pltpu.VMEM((2,) + precursor.shape, f32), pltpu.SemaphoreType.DMA((2, 3)), pltpu.SemaphoreType.DMA((2, 3))],
        compiler_params=pltpu.CompilerParams(vmem_limit_bytes=56 * 1024 * 1024),
    )(*results)


def solution(mesh):
    counts = (mesh.shape["len"], mesh.shape["hgt"], mesh.shape["wid"])
    return jax.shard_map(
        functools.partial(on_device, counts),
        mesh=mesh,
        in_specs=(
            P(None, "len", "hgt", None),
            P(None, "len", "hgt", "wid"),
            P("len", "hgt", "wid"),
            P(None, "hgt"),
            P(None, "hgt"),
        ),
        out_specs=(P(None, "len", "hgt", None), P(None, "len", "hgt", "wid")),
        check_vma=False,
    )
```

```python
import functools

import jax
import jax.numpy as jnp
from jax import lax
from jax.experimental import pallas as pl
from jax.experimental.pallas import tpu as pltpu
from jax.sharding import PartitionSpec as P

STEPS = 3
PARTS = (1, 2)
REMOTE = True

time_step = 0.3
viscosity = 0.04
smag_coef = 0.03
spread_eps = 1e-05


def stencil(u, len_dn, len_up, hgt_dn, hgt_up, wid_dn, wid_up):
    dn, up = (len_dn, hgt_dn, wid_dn), (len_up, hgt_up, wid_up)
    diff = [[up[d][c] - dn[d][c] for d in range(3)] for c in range(3)]
    diag = diff[0][0] * diff[0][0] + diff[1][1] * diff[1][1] + diff[2][2] * diff[2][2]
    s01 = diff[0][1] + diff[1][0]
    s02 = diff[0][2] + diff[2][0]
    s12 = diff[1][2] + diff[2][1]
    total = 2.0 * diag + s01 * s01 + s02 * s02 + s12 * s12
    nu = time_step * viscosity + (0.5 * time_step * smag_coef) * jnp.sqrt(total)
    half = [(0.5 * time_step) * u[d] for d in range(3)]
    out = []
    for c in range(3):
        lap = (up[0][c] + dn[0][c]) + (up[1][c] + dn[1][c]) + (up[2][c] + dn[2][c]) - 6.0 * u[c]
        adv = half[0] * diff[c][0] + half[1] * diff[c][1] + half[2] * diff[c][2]
        out.append(u[c] + nu * lap - adv)
    return out


def kernel(counts, pre_hbm, face_hbm, solid_hbm, prof_hbm, spread_hbm, pre_out, face_out,
           state, solid_ref, prof_ref, spread_ref, hsend, hrecv, wsend, wrecv, load_sem, out_sem, send_sem, recv_sem):
    n_len, n_hgt, n_wid = counts
    planes, rows, cols = solid_ref.shape
    me_len, me_hgt, me_wid = lax.axis_index("len"), lax.axis_index("hgt"), lax.axis_index("wid")
    next_len = lax.rem(me_len + 1, n_len)
    prev_len = lax.rem(me_len + n_len - 1, n_len)

    partners = (
        ("len", next_len, None),
        ("len", prev_len, None),
        ("hgt", me_hgt + 1, me_hgt < n_hgt - 1),
        ("hgt", me_hgt - 1, me_hgt > 0),
        ("wid", me_wid + 1, me_wid < n_wid - 1),
        ("wid", me_wid - 1, me_wid > 0),
    )
    arrives = (None, None, me_hgt > 0, me_hgt < n_hgt - 1, me_wid > 0, me_wid < n_wid - 1)

    def guarded(cond, fn):
        if cond is None:
            fn()
        else:
            pl.when(cond)(fn)

    if REMOTE:
        barrier = pltpu.get_barrier_semaphore()
        for axis, target, cond in partners:
            guarded(cond, lambda axis=axis, target=target: pl.semaphore_signal(
                barrier, inc=1, device_id={axis: target}, device_id_type=pl.DeviceIdType.MESH))

    loads = [
        pltpu.make_async_copy(src, dst, load_sem.at[k])
        for k, (src, dst) in enumerate((
            (pre_hbm, state.at[0, 0, :, 1:planes + 1]),
            (face_hbm, state.at[0, 1, :, 1:planes + 1]),
            (prof_hbm, prof_ref),
            (spread_hbm, spread_ref),
            (solid_hbm, solid_ref),
        ))
    ]
    for copy in loads:
        copy.start()

    sub = lax.broadcasted_iota(jnp.int32, (rows, cols), 0)
    lane = lax.broadcasted_iota(jnp.int32, (rows, cols), 1)

    zero_rows = jnp.zeros(hrecv.shape[3:], jnp.float32)
    zero_cols = jnp.zeros(wrecv.shape[2:], jnp.float32)

    def no_rows(side):
        def go():
            for s in range(STEPS):
                for z in range(2):
                    hrecv[s, z, side] = zero_rows
        return go

    def no_cols(side):
        def go():
            for s in range(STEPS):
                wrecv[s, side] = zero_cols
        return go

    pl.when(me_hgt == 0)(no_rows(0))
    pl.when(me_hgt == n_hgt - 1)(no_rows(1))
    pl.when(me_wid == 0)(no_cols(0))
    pl.when(me_wid == n_wid - 1)(no_cols(1))

    def copies(s, z):
        pairs = [
            (state.at[s, z, :, planes], state.at[s, z, :, 0]),
            (state.at[s, z, :, 1], state.at[s, z, :, planes + 1]),
            (hsend.at[s, z, 1], hrecv.at[s, z, 0]),
            (hsend.at[s, z, 0], hrecv.at[s, z, 1]),
        ]
        if z == 1:
            pairs += [(wsend.at[s], wrecv.at[s, 0]), (wsend.at[s], wrecv.at[s, 1])]
        return [
            pltpu.make_async_remote_copy(
                src_ref=src, dst_ref=dst, send_sem=send_sem.at[s, z, k], recv_sem=recv_sem.at[s, z, k],
                device_id={partners[k][0]: partners[k][1]}, device_id_type=pl.DeviceIdType.MESH)
            for k, (src, dst) in enumerate(pairs)
        ]

    def start(s, z):
        if REMOTE:
            sends = copies(s, z)
            for k in reversed(range(len(sends))):
                guarded(partners[k][2], sends[k].start)

    def wait_recv(s, z):
        if REMOTE:
            for k, copy in enumerate(copies(s, z)):
                guarded(arrives[k], copy.wait_recv)

    def pack(s, z, l, x, acc):
        for c in range(3):
            hsend[s, z, 0, c, pl.ds(l, 1), :] = x[c][0:1]
            hsend[s, z, 1, c, pl.ds(l, 1), :] = x[c][rows - 1:rows]
        if z == 0:
            return acc
        mine = (lane >> 1) == l
        return [jnp.where(mine, pltpu.roll(x[c], 2 * l + 1, 1), acc[c]) for c in range(3)]

    def empty(z):
        return [jnp.zeros((rows, cols), jnp.float32)] * 3 if z == 1 else []

    def send(s, z, acc):
        for c, x in enumerate(acc):
            wsend[s, c] = x
        start(s, z)

    for z in range(2):
        loads[z].wait()

        def first(l, acc, z=z):
            return pack(0, z, l, [state[0, z, c, l + 1] for c in range(3)], acc)

        acc = lax.fori_loop(0, planes, first, empty(z), unroll=True)
        for c, x in enumerate(acc):
            wsend[0, c] = x

    if REMOTE:
        expected = sum([jnp.int32(1) if cond is None else cond.astype(jnp.int32) for _, _, cond in partners])
        pl.semaphore_wait(barrier, expected)
    for z in range(2):
        start(0, z)

    for copy in loads[2:]:
        copy.wait()

    pick = lax.broadcasted_iota(jnp.int32, (rows, rows), 0) == lax.broadcasted_iota(jnp.int32, (rows, rows), 1)

    def column(ref, c):
        return jnp.sum(jnp.where(pick, jnp.broadcast_to(ref[c:c + 1, :], (rows, rows)), 0.0), axis=1, keepdims=True)

    profile = [column(prof_ref, c) for c in range(3)]
    target_spread = [column(spread_ref, c) for c in range(3)]

    def result(z, p):
        part = planes // PARTS[z]
        return pltpu.make_async_copy(
            state.at[STEPS, z, :, p * part + 1:(p + 1) * part + 1],
            (pre_out, face_out)[z].at[:, p * part:(p + 1) * part], out_sem.at[z, p])

    even = (lane & 1) == 0
    for s in range(STEPS):
        for z in range(2):
            if z == 1:
                inlet = []
                for c in range(3):
                    recycled = state[s, 0, c, 0]
                    mean = jnp.sum(recycled, axis=1, keepdims=True) * (1.0 / cols)
                    fluct = recycled - mean
                    var = jnp.sum(fluct * fluct, axis=1, keepdims=True) * (1.0 / cols)
                    inlet.append(profile[c] + target_spread[c] / jnp.sqrt(var + spread_eps) * fluct)
            wait_recv(s, z)
            ghosts = []
            if z == 1:
                for c in range(3):
                    state[s, 1, c, 0] = jnp.where(me_len == 0, inlet[c], state[s, 1, c, 0])
                    state[s, 1, c, planes + 1] = jnp.where(
                        me_len == n_len - 1, state[s, 1, c, planes], state[s, 1, c, planes + 1])
                    ghosts.append(jnp.where(
                        even, pltpu.roll(wrecv[s, 1, c], cols - 1, 1), pltpu.roll(wrecv[s, 0, c], 1, 1)))

            def plane(l, acc, s=s, z=z, ghosts=ghosts):
                u = [state[s, z, c, l + 1] for c in range(3)]
                len_dn = [state[s, z, c, l] for c in range(3)]
                len_up = [state[s, z, c, l + 2] for c in range(3)]
                hgt_dn = [jnp.where(sub == 0, hrecv[s, z, 0, c, pl.ds(l, 1), :], pltpu.roll(u[c], 1, 0)) for c in range(3)]
                hgt_up = [jnp.where(sub == rows - 1, hrecv[s, z, 1, c, pl.ds(l, 1), :], pltpu.roll(u[c], rows - 1, 0)) for c in range(3)]
                edge = [pltpu.roll(ghosts[c], cols - (2 * l + 1), 1) if z == 1 else 0.0 for c in range(3)]
                wid_dn = [jnp.where(lane == 0, edge[c], pltpu.roll(u[c], 1, 1)) for c in range(3)]
                wid_up = [jnp.where(lane == cols - 1, edge[c], pltpu.roll(u[c], cols - 1, 1)) for c in range(3)]
                x = stencil(u, len_dn, len_up, hgt_dn, hgt_up, wid_dn, wid_up)
                if z == 1:
                    share = (1 - solid_ref[l]).astype(jnp.float32)
                    x = [v * share for v in x]
                for c in range(3):
                    state[s + 1, z, c, l + 1] = x[c]
                return acc if s == STEPS - 1 else pack(s + 1, z, l, x, acc)

            if s < STEPS - 1:
                send(s + 1, z, lax.fori_loop(0, planes, plane, empty(z), unroll=True))
            else:
                part = planes // PARTS[z]
                for p in range(PARTS[z]):
                    lax.fori_loop(p * part, (p + 1) * part, plane, empty(z), unroll=True)
                    result(z, p).start()

    for z in range(2):
        for p in range(PARTS[z]):
            result(z, p).wait()
    if REMOTE:
        for s in range(STEPS):
            for z in range(2):
                for k, copy in enumerate(copies(s, z)):
                    guarded(partners[k][2], copy.wait_send)


def copy_kernel(pre_in, face_in, pre_out, face_out, held, in_sem, out_sem):
    pairs = ((pre_in, pre_out), (face_in, face_out))
    loads = [pltpu.make_async_copy(src.at[c], held.at[z, c], in_sem.at[z, c])
             for z, (src, _) in enumerate(pairs) for c in range(3)]
    stores = [pltpu.make_async_copy(held.at[z, c], dst.at[c], out_sem.at[z, c])
              for z, (_, dst) in enumerate(pairs) for c in range(3)]
    for load in loads:
        load.start()
    for load, store in zip(loads, stores):
        load.wait()
        store.start()
    for store in stores:
        store.wait()


def on_device(counts, precursor, face, solid, inlet_profile, target_spread):
    planes, rows, cols = solid.shape
    hbm = pl.BlockSpec(memory_space=pltpu.HBM)
    f32 = jnp.float32
    results = pl.pallas_call(
        functools.partial(kernel, counts),
        out_shape=(jax.ShapeDtypeStruct(precursor.shape, f32), jax.ShapeDtypeStruct(face.shape, f32)),
        in_specs=[hbm] * 5,
        out_specs=(hbm, hbm),
        scratch_shapes=[
            pltpu.VMEM((STEPS + 1, 2, 3, planes + 2, rows, cols), f32),
            pltpu.VMEM(solid.shape, solid.dtype),
            pltpu.VMEM(inlet_profile.shape, f32),
            pltpu.VMEM(target_spread.shape, f32),
            pltpu.VMEM((STEPS, 2, 2, 3, planes, cols), f32),
            pltpu.VMEM((STEPS, 2, 2, 3, planes, cols), f32),
            pltpu.VMEM((STEPS, 3, rows, cols), f32),
            pltpu.VMEM((STEPS, 2, 3, rows, cols), f32),
            pltpu.SemaphoreType.DMA((5,)),
            pltpu.SemaphoreType.DMA((2, 4)),
            pltpu.SemaphoreType.DMA((STEPS, 2, 6)),
            pltpu.SemaphoreType.DMA((STEPS, 2, 6)),
        ],
        compiler_params=pltpu.CompilerParams(
            collective_id=0 if REMOTE else None, has_side_effects=True, vmem_limit_bytes=56 * 1024 * 1024),
    )(precursor, face, solid, inlet_profile, target_spread)
    return pl.pallas_call(
        copy_kernel,
        out_shape=(jax.ShapeDtypeStruct(precursor.shape, f32), jax.ShapeDtypeStruct(face.shape, f32)),
        in_specs=[hbm] * 2,
        out_specs=(hbm, hbm),
        scratch_shapes=[pltpu.VMEM((2,) + precursor.shape, f32), pltpu.SemaphoreType.DMA((2, 3)), pltpu.SemaphoreType.DMA((2, 3))],
        compiler_params=pltpu.CompilerParams(vmem_limit_bytes=56 * 1024 * 1024),
    )(*results)


def solution(mesh):
    counts = (mesh.shape["len"], mesh.shape["hgt"], mesh.shape["wid"])
    return jax.shard_map(
        functools.partial(on_device, counts),
        mesh=mesh,
        in_specs=(
            P(None, "len", "hgt", None),
            P(None, "len", "hgt", "wid"),
            P("len", "hgt", "wid"),
            P(None, "hgt"),
            P(None, "hgt"),
        ),
        out_specs=(P(None, "len", "hgt", None), P(None, "len", "hgt", "wid")),
        check_vma=False,
    )
```

```python
import functools

import jax
import jax.numpy as jnp
from jax import lax
from jax.experimental import pallas as pl
from jax.experimental.pallas import tpu as pltpu
from jax.sharding import PartitionSpec as P

STEPS = 3
PARTS = (1, 2)
REMOTE = True

time_step = 0.3
viscosity = 0.04
smag_coef = 0.03
spread_eps = 1e-05


def stencil(u, len_dn, len_up, hgt_dn, hgt_up, wid_dn, wid_up):
    dn, up = (len_dn, hgt_dn, wid_dn), (len_up, hgt_up, wid_up)
    diff = [[up[d][c] - dn[d][c] for d in range(3)] for c in range(3)]
    diag = diff[0][0] * diff[0][0] + diff[1][1] * diff[1][1] + diff[2][2] * diff[2][2]
    s01 = diff[0][1] + diff[1][0]
    s02 = diff[0][2] + diff[2][0]
    s12 = diff[1][2] + diff[2][1]
    total = 2.0 * diag + s01 * s01 + s02 * s02 + s12 * s12
    nu = time_step * viscosity + (0.5 * time_step * smag_coef) * jnp.sqrt(total)
    half = [(0.5 * time_step) * u[d] for d in range(3)]
    out = []
    for c in range(3):
        lap = (up[0][c] + dn[0][c]) + (up[1][c] + dn[1][c]) + (up[2][c] + dn[2][c]) - 6.0 * u[c]
        adv = half[0] * diff[c][0] + half[1] * diff[c][1] + half[2] * diff[c][2]
        out.append(u[c] + nu * lap - adv)
    return out


def kernel(counts, pre_hbm, face_hbm, solid_hbm, prof_hbm, spread_hbm, pre_out, face_out,
           state, solid_ref, prof_ref, spread_ref, hsend, hrecv, wsend, wrecv, load_sem, out_sem, send_sem, recv_sem):
    n_len, n_hgt, n_wid = counts
    planes, rows, cols = solid_ref.shape
    me_len, me_hgt, me_wid = lax.axis_index("len"), lax.axis_index("hgt"), lax.axis_index("wid")
    next_len = lax.rem(me_len + 1, n_len)
    prev_len = lax.rem(me_len + n_len - 1, n_len)

    partners = (
        ("len", next_len, None),
        ("len", prev_len, None),
        ("hgt", me_hgt + 1, me_hgt < n_hgt - 1),
        ("hgt", me_hgt - 1, me_hgt > 0),
        ("wid", me_wid + 1, me_wid < n_wid - 1),
        ("wid", me_wid - 1, me_wid > 0),
    )
    arrives = (None, None, me_hgt > 0, me_hgt < n_hgt - 1, me_wid > 0, me_wid < n_wid - 1)

    def guarded(cond, fn):
        if cond is None:
            fn()
        else:
            pl.when(cond)(fn)

    if REMOTE:
        barrier = pltpu.get_barrier_semaphore()
        for axis, target, cond in partners:
            guarded(cond, lambda axis=axis, target=target: pl.semaphore_signal(
                barrier, inc=1, device_id={axis: target}, device_id_type=pl.DeviceIdType.MESH))

    loads = [
        pltpu.make_async_copy(src, dst, load_sem.at[k])
        for k, (src, dst) in enumerate((
            (pre_hbm, state.at[0, 0, :, 1:planes + 1]),
            (face_hbm, state.at[0, 1, :, 1:planes + 1]),
            (prof_hbm, prof_ref),
            (spread_hbm, spread_ref),
            (solid_hbm, solid_ref),
        ))
    ]
    for copy in loads:
        copy.start()

    sub = lax.broadcasted_iota(jnp.int32, (rows, cols), 0)
    lane = lax.broadcasted_iota(jnp.int32, (rows, cols), 1)

    zero_rows = jnp.zeros(hrecv.shape[3:], jnp.float32)
    zero_cols = jnp.zeros(wrecv.shape[2:], jnp.float32)

    def no_rows(side):
        def go():
            for s in range(STEPS):
                for z in range(2):
                    hrecv[s, z, side] = zero_rows
        return go

    def no_cols(side):
        def go():
            for s in range(STEPS):
                wrecv[s, side] = zero_cols
        return go

    pl.when(me_hgt == 0)(no_rows(0))
    pl.when(me_hgt == n_hgt - 1)(no_rows(1))
    pl.when(me_wid == 0)(no_cols(0))
    pl.when(me_wid == n_wid - 1)(no_cols(1))

    def copies(s, z):
        pairs = [
            (state.at[s, z, :, planes], state.at[s, z, :, 0]),
            (state.at[s, z, :, 1], state.at[s, z, :, planes + 1]),
            (hsend.at[s, z, 1], hrecv.at[s, z, 0]),
            (hsend.at[s, z, 0], hrecv.at[s, z, 1]),
        ]
        if z == 1:
            pairs += [(wsend.at[s], wrecv.at[s, 0]), (wsend.at[s], wrecv.at[s, 1])]
        return [
            pltpu.make_async_remote_copy(
                src_ref=src, dst_ref=dst, send_sem=send_sem.at[s, z, k], recv_sem=recv_sem.at[s, z, k],
                device_id={partners[k][0]: partners[k][1]}, device_id_type=pl.DeviceIdType.MESH)
            for k, (src, dst) in enumerate(pairs)
        ]

    def start(s, z):
        if REMOTE:
            sends = copies(s, z)
            for k in reversed(range(len(sends))):
                guarded(partners[k][2], sends[k].start)

    def wait_recv(s, z):
        if REMOTE:
            for k, copy in enumerate(copies(s, z)):
                guarded(arrives[k], copy.wait_recv)

    def pack(s, z, l, x, acc):
        for c in range(3):
            hsend[s, z, 0, c, pl.ds(l, 1), :] = x[c][0:1]
            hsend[s, z, 1, c, pl.ds(l, 1), :] = x[c][rows - 1:rows]
        if z == 0:
            return acc
        mine = (lane >> 1) == l
        return [jnp.where(mine, pltpu.roll(x[c], 2 * l + 1, 1), acc[c]) for c in range(3)]

    def empty(z):
        return [jnp.zeros((rows, cols), jnp.float32)] * 3 if z == 1 else []

    def send(s, z, acc):
        for c, x in enumerate(acc):
            wsend[s, c] = x
        start(s, z)

    for z in range(2):
        loads[z].wait()

        def first(l, acc, z=z):
            return pack(0, z, l, [state[0, z, c, l + 1] for c in range(3)], acc)

        acc = lax.fori_loop(0, planes, first, empty(z), unroll=True)
        for c, x in enumerate(acc):
            wsend[0, c] = x

    if REMOTE:
        expected = sum([jnp.int32(1) if cond is None else cond.astype(jnp.int32) for _, _, cond in partners])
        pl.semaphore_wait(barrier, expected)
    for z in range(2):
        start(0, z)

    for copy in loads[2:]:
        copy.wait()

    pick = lax.broadcasted_iota(jnp.int32, (rows, rows), 0) == lax.broadcasted_iota(jnp.int32, (rows, rows), 1)

    def column(ref, c):
        return jnp.sum(jnp.where(pick, jnp.broadcast_to(ref[c:c + 1, :], (rows, rows)), 0.0), axis=1, keepdims=True)

    profile = [column(prof_ref, c) for c in range(3)]
    target_spread = [column(spread_ref, c) for c in range(3)]

    def result(z, p):
        part = planes // PARTS[z]
        return pltpu.make_async_copy(
            state.at[STEPS, z, :, p * part + 1:(p + 1) * part + 1],
            (pre_out, face_out)[z].at[:, p * part:(p + 1) * part], out_sem.at[z, p])

    even = (lane & 1) == 0
    for s in range(STEPS):
        for z in range(2):
            if z == 1:
                inlet = []
                for c in range(3):
                    recycled = state[s, 0, c, 0]
                    mean = jnp.sum(recycled, axis=1, keepdims=True) * (1.0 / cols)
                    fluct = recycled - mean
                    var = jnp.sum(fluct * fluct, axis=1, keepdims=True) * (1.0 / cols)
                    inlet.append(profile[c] + target_spread[c] / jnp.sqrt(var + spread_eps) * fluct)
            wait_recv(s, z)
            ghosts = []
            if z == 1:
                for c in range(3):
                    state[s, 1, c, 0] = jnp.where(me_len == 0, inlet[c], state[s, 1, c, 0])
                    state[s, 1, c, planes + 1] = jnp.where(
                        me_len == n_len - 1, state[s, 1, c, planes], state[s, 1, c, planes + 1])
                    ghosts.append(jnp.where(
                        even, pltpu.roll(wrecv[s, 1, c], cols - 1, 1), pltpu.roll(wrecv[s, 0, c], 1, 1)))

            def plane(l, acc, s=s, z=z, ghosts=ghosts):
                u = [state[s, z, c, l + 1] for c in range(3)]
                len_dn = [state[s, z, c, l] for c in range(3)]
                len_up = [state[s, z, c, l + 2] for c in range(3)]
                hgt_dn = [jnp.where(sub == 0, hrecv[s, z, 0, c, pl.ds(l, 1), :], pltpu.roll(u[c], 1, 0)) for c in range(3)]
                hgt_up = [jnp.where(sub == rows - 1, hrecv[s, z, 1, c, pl.ds(l, 1), :], pltpu.roll(u[c], rows - 1, 0)) for c in range(3)]
                edge = [pltpu.roll(ghosts[c], cols - (2 * l + 1), 1) if z == 1 else 0.0 for c in range(3)]
                wid_dn = [jnp.where(lane == 0, edge[c], pltpu.roll(u[c], 1, 1)) for c in range(3)]
                wid_up = [jnp.where(lane == cols - 1, edge[c], pltpu.roll(u[c], cols - 1, 1)) for c in range(3)]
                x = stencil(u, len_dn, len_up, hgt_dn, hgt_up, wid_dn, wid_up)
                if z == 1:
                    share = (1 - solid_ref[l]).astype(jnp.float32)
                    x = [v * share for v in x]
                for c in range(3):
                    state[s + 1, z, c, l + 1] = x[c]
                return acc if s == STEPS - 1 else pack(s + 1, z, l, x, acc)

            if s < STEPS - 1:
                send(s + 1, z, lax.fori_loop(0, planes, plane, empty(z), unroll=True))
            else:
                part = planes // PARTS[z]
                for p in range(PARTS[z]):
                    lax.fori_loop(p * part, (p + 1) * part, plane, empty(z), unroll=True)
                    result(z, p).start()

    for z in range(2):
        for p in range(PARTS[z]):
            result(z, p).wait()
    if REMOTE:
        for s in range(STEPS):
            for z in range(2):
                for k, copy in enumerate(copies(s, z)):
                    guarded(partners[k][2], copy.wait_send)


def copy_kernel(pre_in, face_in, pre_out, face_out, held, in_sem, out_sem):
    pairs = ((pre_in, pre_out), (face_in, face_out))
    loads = [pltpu.make_async_copy(src, held.at[z], in_sem.at[z, 0]) for z, (src, _) in enumerate(pairs)]
    stores = [pltpu.make_async_copy(held.at[z], dst, out_sem.at[z, 0]) for z, (_, dst) in enumerate(pairs)]
    for load in loads:
        load.start()
    for load, store in zip(loads, stores):
        load.wait()
        store.start()
    for store in stores:
        store.wait()


def on_device(counts, precursor, face, solid, inlet_profile, target_spread):
    planes, rows, cols = solid.shape
    hbm = pl.BlockSpec(memory_space=pltpu.HBM)
    f32 = jnp.float32
    results = pl.pallas_call(
        functools.partial(kernel, counts),
        out_shape=(jax.ShapeDtypeStruct(precursor.shape, f32), jax.ShapeDtypeStruct(face.shape, f32)),
        in_specs=[hbm] * 5,
        out_specs=(hbm, hbm),
        scratch_shapes=[
            pltpu.VMEM((STEPS + 1, 2, 3, planes + 2, rows, cols), f32),
            pltpu.VMEM(solid.shape, solid.dtype),
            pltpu.VMEM(inlet_profile.shape, f32),
            pltpu.VMEM(target_spread.shape, f32),
            pltpu.VMEM((STEPS, 2, 2, 3, planes, cols), f32),
            pltpu.VMEM((STEPS, 2, 2, 3, planes, cols), f32),
            pltpu.VMEM((STEPS, 3, rows, cols), f32),
            pltpu.VMEM((STEPS, 2, 3, rows, cols), f32),
            pltpu.SemaphoreType.DMA((5,)),
            pltpu.SemaphoreType.DMA((2, 4)),
            pltpu.SemaphoreType.DMA((STEPS, 2, 6)),
            pltpu.SemaphoreType.DMA((STEPS, 2, 6)),
        ],
        compiler_params=pltpu.CompilerParams(
            collective_id=0 if REMOTE else None, has_side_effects=True, vmem_limit_bytes=56 * 1024 * 1024),
    )(precursor, face, solid, inlet_profile, target_spread)
    return pl.pallas_call(
        copy_kernel,
        out_shape=(jax.ShapeDtypeStruct(precursor.shape, f32), jax.ShapeDtypeStruct(face.shape, f32)),
        in_specs=[hbm] * 2,
        out_specs=(hbm, hbm),
        scratch_shapes=[pltpu.VMEM((2,) + precursor.shape, f32), pltpu.SemaphoreType.DMA((2, 3)), pltpu.SemaphoreType.DMA((2, 3))],
        compiler_params=pltpu.CompilerParams(vmem_limit_bytes=56 * 1024 * 1024),
    )(*results)


def solution(mesh):
    counts = (mesh.shape["len"], mesh.shape["hgt"], mesh.shape["wid"])
    return jax.shard_map(
        functools.partial(on_device, counts),
        mesh=mesh,
        in_specs=(
            P(None, "len", "hgt", None),
            P(None, "len", "hgt", "wid"),
            P("len", "hgt", "wid"),
            P(None, "hgt"),
            P(None, "hgt"),
        ),
        out_specs=(P(None, "len", "hgt", None), P(None, "len", "hgt", "wid")),
        check_vma=False,
    )
```
